128 devices in a mesh: layer: 16 (over x, z), tile: 8 (over y, core).
Axes of the slice: x: 4, y: 4, z: 4, core: 2. Of those that a mesh axis runs over, the one named last changes fastest.
Arguments:
- source_modes: bfloat16 [16, 8, 2, 64, 512], P('layer', None, None, 'tile'), may hold values from -6 to 6
- port_cells: int32 [8], replicated, may hold values from 0 to 511
- frequencies: float32 [2], replicated, may hold values from 0.3 to 1.5, as said below
- layer_inverse: bfloat16 [16, 2, 64, 512, 512], P('layer', None, 'tile'), may hold values from -0.092807765 to 1.6928078
- coupling_self: float32 [16, 2, 64, 512], P('layer', None, 'tile'), may hold values from 0.4 to 1
- coupling_curl: float32 [16, 2, 64, 512], P('layer', None, 'tile'), may hold values from -4 to 4
Outputs:
- snapshot_basis: float32 [16, 32, 2, 64, 512], P('layer', None, None, 'tile')
- triangle: float32 [32, 32], replicated
The draws below stay inside these ranges and needn't reach their ends.
Inputs may be any that keep to these rules, and one draw needn't show every extreme that they name: `port_cells`: each port's profile is centred on this plane column. `frequencies`: the second frequency is 1.5 to 2.5 times the first.
All inputs are finite; a program needn't handle non-finite values.
Results may differ from the reference program's by a relative error of at most 0.04.
Values may be sent and summed in bfloat16 or wider, within the bound.
No kernel may reach another device: no remote copies, remote signals or barrier semaphores. Data moves between devices by JAX's collectives and lax.ppermute only.
A program may use at most 64 MiB of HBM per device.

```python
import math
import jax
import jax.numpy as jnp
from jax import lax

PW = 512
NPORT = 8
NRHS = 32
NL = 16
PR = 64


def draw_layer_inverse(key, part):
    key_one, key_two = jax.random.split(jax.random.fold_in(key, 11))
    full_shape = (NL, 2, PR, PW, PW)
    jitter = jnp.clip(jax.random.normal(key_one, full_shape, jnp.float32), -4.0, 4.0)
    diagonal = jax.random.uniform(key_two, (NL, 2, PR, PW), jnp.float32, 1.0, 1.5)
    identity = (jnp.arange(PW)[:, None] == jnp.arange(PW)[None, :]).astype(jnp.float32)
    return (jitter * (0.5 / math.sqrt(PW)) + diagonal[..., None] * identity).astype(jnp.bfloat16)


def draw_frequencies(key, part):
    key_one, key_two = jax.random.split(jax.random.fold_in(key, 23))
    base = jnp.exp(jax.random.uniform(key_one, (), jnp.float32, math.log(0.3), math.log(0.6)))
    ratio = jnp.exp(jax.random.uniform(key_two, (), jnp.float32, math.log(1.5), math.log(2.5)))
    return jnp.stack([base, base * ratio]).astype(jnp.float32)


def set_ends(drawn, own_key, low, top_value):
    longest = drawn.shape.index(max(drawn.shape))
    spots = []
    for shift in (0, 1):
        where = [jax.random.randint(jax.random.fold_in(own_key, axis), (), 0, length) for axis, length in enumerate(drawn.shape)]
        where[longest] = (where[longest] + shift) % drawn.shape[longest]
        spots.append(tuple(where))
    return drawn.at[spots[0]].set(low).at[spots[1]].set(top_value)


def levels(stream_key, dims, pieces, smallest, high):
    gain = 1.0
    for axis_at, shards_of in pieces:
        draws = jax.random.uniform(jax.random.fold_in(jax.random.fold_in(stream_key, 6), axis_at), (shards_of,), jnp.float32, smallest / len(pieces), high / len(pieces))
        gain = gain * jnp.repeat(jnp.exp(draws), dims[axis_at] // shards_of).reshape((-1,) + (1,) * (len(dims) - 1 - axis_at))
    return gain


def noise(own_key, extent, scale, most, pieces=(), kind=jnp.bfloat16):
    array = jax.random.normal(own_key, extent, jnp.float32) * scale
    if len(pieces) > 0:
        array = levels(own_key, extent, pieces, -0.22, 0.18) * array
    return jnp.clip(array, min=-most, max=most).astype(kind)


def setup_inputs(seed: int = 0) -> dict:
    arg_keys = jax.random.split(jax.random.key(seed), 7)
    return {
        "source_modes": noise(arg_keys[0], (NL, NPORT, 2, PR, PW), 1.0, 6.0, ((0, 16), (3, 8))),
        "port_cells": set_ends(jax.random.randint(arg_keys[1], (NPORT,), 0, PW), jax.random.fold_in(arg_keys[1], 1), 0, PW - 1).astype(jnp.int32),
        "frequencies": draw_frequencies(jax.random.fold_in(arg_keys[6], 71), 0),
        "layer_inverse": draw_layer_inverse(jax.random.fold_in(arg_keys[6], 71), 0),
        "coupling_self": jnp.clip(0.4 + 0.6 * jax.random.uniform(arg_keys[4], (NL, 2, PR, PW), jnp.float32) ** levels(arg_keys[4], (NL, 2, PR, PW), ((0, 16), (2, 8)), -0.2, 0.2), 0.4, 1.0),
        "coupling_curl": noise(arg_keys[5], (NL, 2, PR, PW), 0.3, 4.0, ((0, 16), (2, 8)), jnp.float32),
    }


def lower_factor(gram):
    order = gram.shape[0]
    index_row = jnp.arange(order)

    def column_step(col_no, lower):
        unit = (index_row == col_no).astype(gram.dtype)
        column = jnp.dot(gram, unit, precision=lax.Precision.HIGHEST)
        lower_row = jnp.dot(unit, lower, precision=lax.Precision.HIGHEST)
        column = column - jnp.dot(lower, lower_row, precision=lax.Precision.HIGHEST)
        pivot = jnp.sqrt(jnp.sum(column * unit))
        scaled = jnp.where(index_row >= col_no, column / pivot, 0.0)
        return lower + scaled[:, None] * unit[None, :]
    return lax.fori_loop(0, order, column_step, jnp.zeros_like(gram))

def lower_inverse(lower):
    order = lower.shape[0]
    index_row = jnp.arange(order)

    def row_step(row_no, inverse):
        unit = (index_row == row_no).astype(lower.dtype)
        lower_row = jnp.dot(unit, lower, precision=lax.Precision.HIGHEST)
        pivot = jnp.sum(lower_row * unit)
        new_row = (unit - jnp.dot(lower_row, inverse, precision=lax.Precision.HIGHEST)) / pivot
        return inverse + unit[:, None] * new_row[None, :]
    return lax.fori_loop(0, order, row_step, jnp.zeros_like(lower))

def couple(field, self_w, curl_w):
    x_part = field[:, 0]
    y_part = field[:, 1]
    rows_pad = jnp.pad(y_part, ((0, 0), (1, 1), (0, 0)))
    row_diff = rows_pad[:, 2:] - rows_pad[:, :-2]
    cols_pad = jnp.pad(x_part, ((0, 0), (0, 0), (1, 1)))
    col_diff = cols_pad[:, :, 2:] - cols_pad[:, :, :-2]
    part_one = self_w[0] * x_part + curl_w[0] * row_diff
    part_two = self_w[1] * y_part + curl_w[1] * col_diff
    return jnp.stack([part_one, part_two], axis=1)

def apply_inverse(inverse_block, vectors):
    return jnp.einsum('crik,jcrk->jcri', inverse_block.astype(jnp.float32), vectors.astype(jnp.float32), precision=lax.Precision.HIGHEST)

def excitation(source_layer, port_taper, phase_pair):
    full_field = source_layer.astype(jnp.float32)[:, None, None] * port_taper[:, None, None, None, None, :] * phase_pair[None, :, :, None, None, None]
    return full_field.reshape((-1,) + source_layer.shape[1:])

def reference(source_modes, port_cells, frequencies, layer_inverse, coupling_self, coupling_curl):
    columns = jnp.arange(PW, dtype=jnp.float32)
    offsets = (columns[None, :] - port_cells.astype(jnp.float32)[:, None]) / (PW // 8)
    port_taper = 1.0 / (1.0 + offsets * offsets)
    down_list = []
    previous = jnp.zeros((NRHS, 2, PR, PW), jnp.bfloat16)
    for layer_no in range(NL):
        phase_angle = frequencies * (layer_no + 1.0)
        phase_pair = jnp.stack([jnp.cos(phase_angle), jnp.sin(phase_angle)], axis=1)
        forcing = excitation(source_modes[layer_no], port_taper, phase_pair)
        residue = (forcing - couple(previous.astype(jnp.float32), coupling_self[layer_no], coupling_curl[layer_no])).astype(jnp.bfloat16)
        current = apply_inverse(layer_inverse[layer_no], residue).astype(jnp.bfloat16)
        down_list.append(current)
        previous = current
    up_list = [None] * NL
    following = jnp.zeros((NRHS, 2, PR, PW), jnp.float32)
    for layer_no in range(NL - 1, -1, -1):
        up_image = couple(following, coupling_self[layer_no], coupling_curl[layer_no]).astype(jnp.bfloat16)
        update = apply_inverse(layer_inverse[layer_no], up_image)
        current = down_list[layer_no].astype(jnp.float32) - update
        up_list[layer_no] = current
        following = current
    snapshots = jnp.stack(up_list)
    columns_mat = jnp.moveaxis(snapshots, 1, 0).reshape(NRHS, -1)
    gram_whole = jnp.dot(columns_mat, columns_mat.T, precision=lax.Precision.HIGHEST)
    total_rows = NL * 2 * PR * PW
    lower = lower_factor(gram_whole / total_rows)
    triangle = lower.T
    solved = jnp.dot(lower_inverse(lower), columns_mat, precision=lax.Precision.HIGHEST)
    snapshot_basis = jnp.moveaxis(solved.reshape(NRHS, NL, 2, PR, PW), 0, 1)
    return (snapshot_basis, triangle)
```

```python
import functools

import jax
import jax.numpy as jnp
from jax import lax
from jax.experimental import pallas as pl
from jax.experimental.pallas import tpu as pltpu
from jax.sharding import PartitionSpec as P

AXES = ("layer", "tile")
BF16 = jnp.bfloat16
F32 = jnp.float32
NL = 16
NY = 4
W = 512
NJ = 32
EXTRA = 16
BLOCK = W + EXTRA
VMEM = pl.BlockSpec(memory_space=pltpu.VMEM)
SMEM = pl.BlockSpec(memory_space=pltpu.SMEM)
ANY = pl.BlockSpec(memory_space=pl.ANY)
PARAMS = pltpu.CompilerParams(vmem_limit_bytes=24 * 1024 * 1024)


def spot(row, y):
    rank = row + (y % 2) * (NL - 1 - 2 * row)
    x, z = rank // 4, rank % 4
    return 4 * x + z + (x % 2) * (3 - 2 * z)


def device_of(row, comp):
    y = row // NL
    return spot(row % NL, y) * 2 * NY + 2 * y + comp


ROWS = NL * NY
CORE = [(device_of(r, c), device_of(r, 1 - c)) for r in range(ROWS) for c in range(2)]
RAISE = [(device_of(r, c), device_of((r + 1) % ROWS, 1 - c)) for r in range(ROWS) for c in range(2)]
LOWER = [(device_of(r, c), device_of((r - 1) % ROWS, 1 - c)) for r in range(ROWS) for c in range(2)]


def swap(value, pairs):
    return lax.ppermute(value, AXES, pairs)


def exchanges():
    rounds = [[(d, d ^ 1) for d in range(128)]]
    for bit in (1, 3, 5):
        size = 1 << bit
        for odd in (0, 1):
            pairs = []
            for d in range(128):
                at = (d // size) % 4
                to = at ^ 1 if odd == 0 else (at + 1 if at % 2 else at - 1) % 4
                pairs.append((d, d + (to - at) * size))
            rounds.append(pairs)
    return rounds


def pack_send(place, blocks, extras, out):
    out[0, 0:W, :] = blocks[0, 0, 0]
    out[0, W:BLOCK, :] = extras[0, 0]


def pack_other(place, received, part, out):
    out[0] = received[0]


def half_specs(other):
    def comp(place):
        return 1 - place[0] if other else place[0]

    return [
        pl.BlockSpec((1, 1, 1, W, W), lambda i, place: (0, comp(place), i, 0, 0)),
        pl.BlockSpec((1, 1, EXTRA, W), lambda i, place: (comp(place), i, 0, 0)),
    ]


def spot_spec(other):
    def index(i, place):
        core = 1 - place[0] if other else place[0]
        return (spot(8 * core + i, place[1]), 0, 0)

    return pl.BlockSpec((1, BLOCK, W), index)


def eight(kernel, out_rows, in_specs, out_spec, place, *arrays, **options):
    return pl.pallas_call(
        kernel,
        out_shape=jax.ShapeDtypeStruct((out_rows, BLOCK, W), BF16),
        grid_spec=pltpu.PrefetchScalarGridSpec(
            num_scalar_prefetch=1, grid=(8,), in_specs=in_specs, out_specs=out_spec
        ),
        **options,
    )(place, *arrays)


def apply_block(vectors, blocks, layer):
    return lax.dot_general(
        vectors, blocks[layer], (((1,), (1,)), ((), ())), preferred_element_type=F32
    )


def couple(coef, layer, own, diff):
    return coef[layer, 0:1, :] * own + coef[layer, 1:2, :] * diff


def start_kernel(blocks, forcing, down, send):
    current = apply_block(forcing[0].astype(BF16), blocks, 0).astype(BF16)
    down[0] = current
    send[...] = current


def phase_kernel(comp, steps, place, blocks, forcing, coef, *refs):
    near = refs[0:1] if comp == 1 else refs[0:2]
    down_in, up_in, down, up, send = refs[len(near):]
    columns = lax.broadcasted_iota(jnp.int32, (NJ, W), 1)

    def differences(slot):
        if comp == 1:
            field = near[0][slot].astype(F32)
            after = jnp.where(columns == W - 1, 0.0, pltpu.roll(field, W - 1, 1))
            before = jnp.where(columns == 0, 0.0, pltpu.roll(field, 1, 1))
            return after - before
        below = jnp.where(place[2] == 0, 0.0, near[0][slot].astype(F32))
        above = jnp.where(place[2] == ROWS - 1, 0.0, near[1][slot].astype(F32))
        return above - below

    @pl.when(place[0] == comp)
    def _():
        for slot, (layer, is_up) in enumerate(steps):
            diff = differences(slot)
            if is_up:
                own = down[layer + 1].astype(F32) if layer == NL - 2 else up[layer + 1]
                image = couple(coef, layer, own, diff).astype(BF16)
                current = down[layer].astype(F32) - apply_block(image, blocks, layer)
                up[layer] = current
                send[slot] = current.astype(BF16)
            else:
                own = down[layer - 1].astype(F32)
                residue = (forcing[layer] - couple(coef, layer, own, diff)).astype(BF16)
                current = apply_block(residue, blocks, layer).astype(BF16)
                down[layer] = current
                send[slot] = current
                if layer == NL - 1:
                    up[layer] = current.astype(F32)

    @pl.when(place[0] != comp)
    def _():
        send[...] = jnp.zeros_like(send)


def phase(comp, steps, place, blocks, forcing, coef, near, down, up):
    first = 4 + len(near)
    return pl.pallas_call(
        functools.partial(phase_kernel, comp, steps),
        out_shape=(
            jax.ShapeDtypeStruct(down.shape, down.dtype),
            jax.ShapeDtypeStruct(up.shape, up.dtype),
            jax.ShapeDtypeStruct((len(steps), NJ, W), BF16),
        ),
        in_specs=[SMEM] + [VMEM] * (5 + len(near)),
        out_specs=(VMEM, VMEM, VMEM),
        input_output_aliases={first: 0, first + 1: 1},
        compiler_params=PARAMS,
    )(place, blocks, forcing, coef, *near, down, up)


def gram_kernel(up, gram):
    total = jnp.zeros((NJ, NJ), F32)
    for layer in range(NL):
        rows = up[layer]
        total += lax.dot_general(
            rows, rows, (((1,), (1,)), ((), ())),
            precision=lax.Precision.HIGHEST, preferred_element_type=F32,
        )
    gram[...] = total


def factor_kernel(gram, up, basis, triangle):
    lane = lax.broadcasted_iota(jnp.int32, (NJ, NJ), 1)
    row = lax.broadcasted_iota(jnp.int32, (NJ, NJ), 0)
    left = gram[...] * (1.0 / (NL * 2 * ROWS * W))
    right = jnp.where(lane == row, 1.0, 0.0)
    for k in range(NJ):
        scale = lax.rsqrt(left[k:k + 1, k:k + 1])
        row_left = left[k:k + 1, :] * scale
        row_right = right[k:k + 1, :] * scale
        factor = jnp.where(row > k, left[:, k:k + 1] * scale, 0.0)
        left = jnp.where(row == k, row_left, left - factor * row_left)
        right = jnp.where(row == k, row_right, right - factor * row_right)
    triangle[...] = jnp.where(lane >= row, left, 0.0)
    for layer in range(NL):
        basis[layer] = jnp.dot(
            right, up[layer], precision=lax.Precision.HIGHEST, preferred_element_type=F32
        ).astype(BF16)


def unpack_send(place, rows, send):
    core, y = place[0], place[1]
    for i in range(8):
        send[i] = rows[spot(8 * (1 - core) + i, y)]


def unpack_all(place, rows, received, out):
    core, y = place[0], place[1]
    for i in range(8):
        own = rows[spot(8 * core + i, y)].astype(F32)
        other = received[i].astype(F32)
        out[0, :, 0, i, :] = jnp.where(core == 0, own, other)
        out[0, :, 1, i, :] = jnp.where(core == 0, other, own)


def per_device(source_modes, port_cells, frequencies, layer_inverse, coupling_self, coupling_curl):
    layer_pos = lax.axis_index("layer")
    tile = lax.axis_index("tile")
    core, y = tile % 2, tile // 2
    x, z = layer_pos // 4, layer_pos % 4
    rank = 4 * x + jnp.where(x % 2 == 0, z, 3 - z)
    row = NL * y + jnp.where(y % 2 == 0, rank, NL - 1 - rank)
    place = jnp.stack([core, y, row, jnp.zeros_like(row)]).astype(jnp.int32)

    def pieces(values):
        out = []
        for _ in range(3):
            part = lax.reduce_precision(values, 8, 7)
            out.append(part.astype(BF16))
            values = values - part
        return out

    extras = jnp.concatenate(
        [jnp.moveaxis(source_modes[0], 0, 2)]
        + [p[:, :, None] for p in pieces(coupling_self[0]) + pieces(coupling_curl[0])]
        + [jnp.zeros((2, 8, EXTRA - 14, W), BF16)],
        axis=2,
    )
    in_turn = pl.BlockSpec((1, BLOCK, W), lambda i, place: (i, 0, 0))
    to_send = eight(pack_send, 8, half_specs(True), in_turn, place, layer_inverse, extras)
    received = swap(to_send, CORE)
    part = eight(pack_send, NL, half_specs(False), spot_spec(False), place, layer_inverse, extras)
    packed = eight(
        pack_other, NL, [in_turn, ANY], spot_spec(True), place, received, part,
        input_output_aliases={2: 0},
    )
    arrived = lax.all_to_all(packed, "layer", 0, 0, tiled=True)
    blocks = arrived[:, 0:W]

    columns = jnp.arange(W, dtype=F32)
    offsets = (columns[None, :] - port_cells.astype(F32)[:, None]) / (W // 8)
    port_taper = 1.0 / (1.0 + offsets * offsets)
    angle = frequencies[None, :] * (jnp.arange(NL, dtype=F32)[:, None] + 1.0)
    phases = jnp.stack([jnp.cos(angle), jnp.sin(angle)], axis=2)
    sources = arrived[:, W:W + 8].astype(F32)
    forcing = (
        sources[:, :, None, None]
        * port_taper[None, :, None, None, :]
        * phases[:, None, :, :, None]
    ).reshape(NL, NJ, W)
    coupling = arrived[:, W + 8:W + 14].astype(F32)
    coef = jnp.stack(
        [coupling[:, 0] + coupling[:, 1] + coupling[:, 2], coupling[:, 3] + coupling[:, 4] + coupling[:, 5]],
        axis=1,
    )

    down, first = pl.pallas_call(
        start_kernel,
        out_shape=(jax.ShapeDtypeStruct((NL, NJ, W), BF16), jax.ShapeDtypeStruct((NJ, W), BF16)),
        in_specs=[VMEM, VMEM],
        out_specs=(VMEM, VMEM),
        compiler_params=PARAMS,
    )(blocks, forcing)
    up = jnp.zeros((NL, NJ, W), F32)

    sequence = [(layer, False) for layer in range(NL)] + [(layer, True) for layer in range(NL - 2, -1, -1)]
    run = lambda comp, at, near, down, up: phase(
        comp, sequence[at[0]:at[1]], place, blocks, forcing, coef, near, down, up
    )
    x_sent = swap(first, CORE)[None]
    down, up, y_new = run(1, (1, 2), [x_sent], down, up)
    y_pair = jnp.concatenate([first[None], y_new])
    at = 1
    last = len(sequence)
    while at < last:
        stop = min(at + 2, last)
        near = [swap(y_pair, RAISE), swap(y_pair, LOWER)]
        down, up, x_pair = run(0, (at, stop), near, down, up)
        y_stop = min(at + 3, last)
        x_sent = swap(x_pair[:y_stop - at - 1], CORE)
        down, up, y_pair = run(1, (at + 1, y_stop), [x_sent], down, up)
        at = stop

    gram = pl.pallas_call(
        gram_kernel,
        out_shape=jax.ShapeDtypeStruct((NJ, NJ), F32),
        in_specs=[VMEM],
        out_specs=VMEM,
        compiler_params=PARAMS,
    )(up)
    for pairs in exchanges():
        gram = gram + swap(gram, pairs)
    basis, triangle = pl.pallas_call(
        factor_kernel,
        out_shape=(jax.ShapeDtypeStruct((NL, NJ, W), BF16), jax.ShapeDtypeStruct((NJ, NJ), F32)),
        in_specs=[VMEM, VMEM],
        out_specs=(VMEM, VMEM),
        compiler_params=PARAMS,
    )(gram, up)
    rows = lax.all_to_all(basis, "layer", 0, 0, tiled=True)
    back = pl.pallas_call(
        unpack_send,
        out_shape=jax.ShapeDtypeStruct((8, NJ, W), BF16),
        in_specs=[SMEM, VMEM],
        out_specs=VMEM,
        compiler_params=PARAMS,
    )(place, rows)
    out = pl.pallas_call(
        unpack_all,
        out_shape=jax.ShapeDtypeStruct((1, NJ, 2, 8, W), F32),
        in_specs=[SMEM, VMEM, VMEM],
        out_specs=VMEM,
        compiler_params=PARAMS,
    )(place, rows, swap(back, CORE))
    return (out, triangle)


def solution(mesh):
    in_specs = (
        P("layer", None, None, "tile", None),
        P(),
        P(),
        P("layer", None, "tile", None, None),
        P("layer", None, "tile", None),
        P("layer", None, "tile", None),
    )
    out_specs = (P("layer", None, None, "tile", None), P())
    return jax.shard_map(
        per_device, mesh=mesh, in_specs=in_specs, out_specs=out_specs, check_vma=False
    )
```

```python
import functools

import jax
import jax.numpy as jnp
from jax import lax
from jax.experimental import pallas as pl
from jax.experimental.pallas import tpu as pltpu
from jax.sharding import PartitionSpec as P

AXES = ("layer", "tile")
BF16 = jnp.bfloat16
F32 = jnp.float32
NL = 16
NY = 4
W = 512
NJ = 32
EXTRA = 16
BLOCK = W + EXTRA
TAIL = 128
VMEM = pl.BlockSpec(memory_space=pltpu.VMEM)
SMEM = pl.BlockSpec(memory_space=pltpu.SMEM)
ANY = pl.BlockSpec(memory_space=pl.ANY)
ALONE = pltpu.CompilerParams(vmem_limit_bytes=57 * 1024 * 1024)
PARAMS = pltpu.CompilerParams(vmem_limit_bytes=24 * 1024 * 1024)


def spot(row, y):
    rank = row + (y % 2) * (NL - 1 - 2 * row)
    x, z = rank // 4, rank % 4
    return 4 * x + z + (x % 2) * (3 - 2 * z)


def device_of(row, comp):
    y = row // NL
    return spot(row % NL, y) * 2 * NY + 2 * y + comp


ROWS = NL * NY
CORE = [(device_of(r, c), device_of(r, 1 - c)) for r in range(ROWS) for c in range(2)]
RAISE = [(device_of(r, c), device_of((r + 1) % ROWS, 1 - c)) for r in range(ROWS) for c in range(2)]
LOWER = [(device_of(r, c), device_of((r - 1) % ROWS, 1 - c)) for r in range(ROWS) for c in range(2)]


def swap(value, pairs):
    return lax.ppermute(value, AXES, pairs)


def exchanges():
    devices = range(NL * 2 * NY)
    even = [(d, d ^ 2) for d in devices]
    odd = [(d, d - d % 8 + (d + (2 if d & 2 else 6)) % 8) for d in devices]
    return [[(d, d ^ 1) for d in devices], even, odd]


def start_all(copies):
    for copy in copies:
        copy.start()
    return copies


def wait_all(copies):
    for copy in copies:
        copy.wait()


def pack_send(place, blocks, send, held, sems):
    entering = start_all([
        pltpu.make_async_copy(blocks.at[0, 1 - place[0], i], held.at[i], sems.at[i]) for i in range(8)
    ])
    leaving = []
    for i in range(8):
        entering[i].wait()
        leaving += start_all([pltpu.make_async_copy(held.at[i], send.at[i], sems.at[8 + i])])
    wait_all(leaving)


def pack_all(place, blocks, extras, received, more, phases, taper, out, phases_out, taper_out, sems):
    core, y = place[0], place[1]
    copies = []
    for i in range(8):
        own, other = spot(8 * core + i, y), spot(8 * (1 - core) + i, y)
        copies += start_all([
            pltpu.make_async_copy(blocks.at[0, core, i], out.at[own, pl.ds(0, W)], sems.at[i]),
            pltpu.make_async_copy(received.at[i], out.at[other, pl.ds(0, W)], sems.at[8 + i]),
        ])
    for i in range(8):
        own, other = spot(8 * core + i, y), spot(8 * (1 - core) + i, y)
        out[own, W:BLOCK, :] = extras[core, i]
        out[other, W:BLOCK, :] = more[i]
    phases_out[...] = phases[...]
    taper_out[...] = taper[...]
    wait_all(copies)


def apply_block(vectors, blocks, layer):
    return lax.dot_general(
        vectors, blocks[layer], (((1,), (1,)), ((), ())), preferred_element_type=F32
    )


def couple(coef, layer, own, diff):
    return coef[layer, 0:1, :] * own + coef[layer, 1:2, :] * diff


def start_kernel(phases, taper, arrived, blocks, forcing, coef, down, up, send, extras, sems):
    edge = pltpu.make_async_copy(arrived.at[:, pl.ds(W, EXTRA)], extras, sems.at[NL])
    edge.start()
    copies = []
    for layer in range(NL):
        copies.append(pltpu.make_async_copy(arrived.at[layer, pl.ds(0, W)], blocks.at[layer], sems.at[layer]))
        copies[layer].start()
    edge.wait()
    for layer in range(NL):
        rows = extras[layer].astype(F32)
        shaped = rows[0:8] * taper[...]
        for m in range(4):
            forcing[layer, 8 * m:8 * m + 8, :] = shaped * phases[layer, m]
        coef[layer, 0:1, :] = rows[8:9] + rows[9:10] + rows[10:11]
        coef[layer, 1:2, :] = rows[11:12] + rows[12:13] + rows[13:14]
    copies[0].wait()
    current = apply_block(forcing[0].astype(BF16), blocks, 0).astype(BF16)
    down[0] = current
    send[0] = current
    for layer in range(1, NL):
        copies[layer].wait()


def phase_kernel(comp, steps, place, blocks, forcing, coef, *refs):
    near = refs[0:1] if comp == 1 else refs[0:2]
    down_in, up_in, down, up, send = refs[len(near):]
    columns = lax.broadcasted_iota(jnp.int32, (NJ, W), 1)

    def differences(slot):
        if comp == 1:
            field = near[0][slot].astype(F32)
            after = jnp.where(columns == W - 1, 0.0, pltpu.roll(field, W - 1, 1))
            before = jnp.where(columns == 0, 0.0, pltpu.roll(field, 1, 1))
            return after - before
        below = jnp.where(place[2] == 0, 0.0, near[0][slot].astype(F32))
        above = jnp.where(place[2] == ROWS - 1, 0.0, near[1][slot].astype(F32))
        return above - below

    @pl.when(place[0] == comp)
    def _():
        for slot, (layer, is_up) in enumerate(steps):
            diff = differences(slot)
            if is_up:
                own = down[layer + 1].astype(F32) if layer == NL - 2 else up[layer + 1]
                image = couple(coef, layer, own, diff).astype(BF16)
                current = down[layer].astype(F32) - apply_block(image, blocks, layer)
                up[layer] = current
                send[slot] = current.astype(BF16)
            else:
                own = down[layer - 1].astype(F32)
                residue = (forcing[layer] - couple(coef, layer, own, diff)).astype(BF16)
                current = apply_block(residue, blocks, layer).astype(BF16)
                down[layer] = current
                send[slot] = current
                if layer == NL - 1:
                    up[layer] = current.astype(F32)

    @pl.when(place[0] != comp)
    def _():
        send[...] = jnp.zeros_like(send)


def phase(comp, steps, place, blocks, forcing, coef, near, down, up):
    first = 4 + len(near)
    return pl.pallas_call(
        functools.partial(phase_kernel, comp, steps),
        out_shape=(
            jax.ShapeDtypeStruct(down.shape, down.dtype),
            jax.ShapeDtypeStruct(up.shape, up.dtype),
            jax.ShapeDtypeStruct((len(steps), NJ, W), BF16),
        ),
        in_specs=[SMEM] + [VMEM] * (5 + len(near)),
        out_specs=(VMEM, VMEM, VMEM),
        input_output_aliases={first: 0, first + 1: 1},
        compiler_params=PARAMS,
    )(place, blocks, forcing, coef, *near, down, up)


def pieces(values):
    out = []
    for _ in range(3):
        part = values.astype(BF16)
        out.append(part)
        values = values - part.astype(F32)
    return out


def gram_kernel(up, send):
    total = jnp.zeros((NJ, NJ), F32)
    for layer in range(NL):
        rows = up[layer]
        total += lax.dot_general(
            rows, rows, (((1,), (1,)), ((), ())),
            precision=lax.Precision.HIGHEST, preferred_element_type=F32,
        )
        send[layer, :, 0:W] = rows.astype(BF16)
    tail = jnp.concatenate(pieces(total) + [jnp.zeros((NJ, NJ), BF16)], axis=1)
    for layer in range(NL):
        send[layer, :, W:W + TAIL] = tail


def collect_kernel(place, rows, gram, send):
    total = jnp.zeros((NJ, TAIL), F32)
    for at in range(NL):
        total += rows[at, :, W:W + TAIL].astype(F32)
    gram[...] = total[:, 0:NJ] + total[:, NJ:2 * NJ] + total[:, 2 * NJ:3 * NJ]
    for i in range(8):
        send[i] = rows[spot(8 * (1 - place[0]) + i, place[1]), :, 0:W]


def final_kernel(place, gram, rows, received, out, triangle):
    lane = lax.broadcasted_iota(jnp.int32, (NJ, NJ), 1)
    row = lax.broadcasted_iota(jnp.int32, (NJ, NJ), 0)
    order = jnp.where(lane == (row % 4) * 8 + row // 4, 1.0, 0.0)
    back = jnp.where(row == (lane % 4) * 8 + lane // 4, 1.0, 0.0)
    exact = functools.partial(jnp.dot, precision=lax.Precision.HIGHEST, preferred_element_type=F32)
    left = exact(exact(order, gram[...] * (1.0 / (NL * 2 * ROWS * W))), back)
    right = order
    for k in range(NJ):
        scale = lax.rsqrt(left[k:k + 1, k:k + 1])
        row_left = left[k:k + 1, :] * scale
        row_right = right[k:k + 1, :] * scale
        factor = jnp.where(row > k, left[:, k:k + 1] * scale, 0.0)
        left = jnp.where(row == k, row_left, left - factor * row_left)
        right = jnp.where(row == k, row_right, right - factor * row_right)
    triangle[...] = jnp.where(lane >= row, left, 0.0)
    core, y = place[0], place[1]
    for i in range(8):
        own = exact(right, rows[spot(8 * core + i, y), :, 0:W].astype(F32))
        other = exact(right, received[i].astype(F32))
        out[0, :, 0, i, :] = jnp.where(core == 0, own, other)
        out[0, :, 1, i, :] = jnp.where(core == 0, other, own)


def per_device(source_modes, port_cells, frequencies, layer_inverse, coupling_self, coupling_curl):
    layer_pos = lax.axis_index("layer")
    tile = lax.axis_index("tile")
    core, y = tile % 2, tile // 2
    x, z = layer_pos // 4, layer_pos % 4
    rank = 4 * x + jnp.where(x % 2 == 0, z, 3 - z)
    row = NL * y + jnp.where(y % 2 == 0, rank, NL - 1 - rank)
    place = jnp.stack([core, y, row, jnp.zeros_like(row)]).astype(jnp.int32)

    def split(values):
        out = []
        for _ in range(3):
            part = lax.reduce_precision(values, 8, 7)
            out.append(part.astype(BF16))
            values = values - part
        return out

    extras = jnp.concatenate(
        [jnp.moveaxis(source_modes[0], 0, 2)]
        + [p[:, :, None] for p in split(coupling_self[0]) + split(coupling_curl[0])]
        + [jnp.zeros((2, 8, EXTRA - 14, W), BF16)],
        axis=2,
    )
    columns = jnp.arange(W, dtype=F32)
    offsets = (columns[None, :] - port_cells.astype(F32)[:, None]) / (W // 8)
    port_taper = 1.0 / (1.0 + offsets * offsets)
    angle = frequencies[None, :] * (jnp.arange(NL, dtype=F32)[:, None] + 1.0)
    phases = jnp.stack([jnp.cos(angle), jnp.sin(angle)], axis=2).reshape(NL, 4)
    to_send = pl.pallas_call(
        pack_send,
        out_shape=jax.ShapeDtypeStruct((8, W, W), BF16),
        in_specs=[SMEM, ANY],
        out_specs=ANY,
        scratch_shapes=[pltpu.VMEM((8, W, W), BF16), pltpu.SemaphoreType.DMA((16,))],
        compiler_params=ALONE,
    )(place, layer_inverse)
    received = swap(to_send, CORE)
    more = swap(lax.dynamic_index_in_dim(extras, 1 - core, 0, keepdims=False), CORE)
    packed, phases, port_taper = pl.pallas_call(
        pack_all,
        out_shape=(
            jax.ShapeDtypeStruct((NL, BLOCK, W), BF16),
            jax.ShapeDtypeStruct(phases.shape, F32),
            jax.ShapeDtypeStruct(port_taper.shape, F32),
        ),
        in_specs=[SMEM, ANY, VMEM, ANY, VMEM, VMEM, VMEM],
        out_specs=(VMEM, VMEM, VMEM),
        scratch_shapes=[pltpu.SemaphoreType.DMA((16,))],
        compiler_params=PARAMS,
    )(place, layer_inverse, extras, received, more, phases, port_taper)
    arrived = lax.all_to_all(packed, "layer", 0, 0, tiled=True)

    blocks, forcing, coef, down, up, first = pl.pallas_call(
        start_kernel,
        out_shape=(
            jax.ShapeDtypeStruct((NL, W, W), BF16),
            jax.ShapeDtypeStruct((NL, NJ, W), F32),
            jax.ShapeDtypeStruct((NL, 2, W), F32),
            jax.ShapeDtypeStruct((NL, NJ, W), BF16),
            jax.ShapeDtypeStruct((NL, NJ, W), F32),
            jax.ShapeDtypeStruct((1, NJ, W), BF16),
        ),
        in_specs=[SMEM, VMEM, ANY],
        out_specs=(VMEM,) * 6,
        scratch_shapes=[pltpu.VMEM((NL, EXTRA, W), BF16), pltpu.SemaphoreType.DMA((NL + 1,))],
        compiler_params=PARAMS,
    )(phases, port_taper, arrived)

    sequence = [(layer, False) for layer in range(NL)] + [(layer, True) for layer in range(NL - 2, -1, -1)]
    run = lambda comp, at, near, down, up: phase(
        comp, sequence[at[0]:at[1]], place, blocks, forcing, coef, near, down, up
    )
    x_sent = swap(first, CORE)
    down, up, y_new = run(1, (1, 2), [x_sent], down, up)
    y_pair = jnp.concatenate([first, y_new])
    at = 1
    last = len(sequence)
    while at < last:
        stop = min(at + 2, last)
        near = [swap(y_pair, RAISE), swap(y_pair, LOWER)]
        down, up, x_pair = run(0, (at, stop), near, down, up)
        y_stop = min(at + 3, last)
        x_sent = swap(x_pair[:y_stop - at - 1], CORE)
        down, up, y_pair = run(1, (at + 1, y_stop), [x_sent], down, up)
        at = stop

    basis = pl.pallas_call(
        gram_kernel,
        out_shape=jax.ShapeDtypeStruct((NL, NJ, W + TAIL), BF16),
        in_specs=[VMEM],
        out_specs=VMEM,
        compiler_params=PARAMS,
    )(up)
    rows = lax.all_to_all(basis, "layer", 0, 0, tiled=True)
    gram, back = pl.pallas_call(
        collect_kernel,
        out_shape=(jax.ShapeDtypeStruct((NJ, NJ), F32), jax.ShapeDtypeStruct((8, NJ, W), BF16)),
        in_specs=[SMEM, VMEM],
        out_specs=(VMEM, VMEM),
        compiler_params=PARAMS,
    )(place, rows)
    received = swap(back, CORE)
    for pairs in exchanges():
        gram = gram + swap(gram, pairs)
    out, triangle = pl.pallas_call(
        final_kernel,
        out_shape=(
            jax.ShapeDtypeStruct((1, NJ, 2, 8, W), F32),
            jax.ShapeDtypeStruct((NJ, NJ), F32),
        ),
        in_specs=[SMEM, VMEM, VMEM, VMEM],
        out_specs=(VMEM, VMEM),
        compiler_params=PARAMS,
    )(place, gram, rows, received)
    return (out, triangle)


def solution(mesh):
    in_specs = (
        P("layer", None, None, "tile", None),
        P(),
        P(),
        P("layer", None, "tile", None, None),
        P("layer", None, "tile", None),
        P("layer", None, "tile", None),
    )
    out_specs = (P("layer", None, None, "tile", None), P())
    return jax.shard_map(
        per_device, mesh=mesh, in_specs=in_specs, out_specs=out_specs, check_vma=False
    )
```

```python
import functools

import jax
import jax.numpy as jnp
from jax import lax
from jax.experimental import pallas as pl
from jax.experimental.pallas import tpu as pltpu
from jax.sharding import PartitionSpec as P

AXES = ("layer", "tile")
BF16 = jnp.bfloat16
F32 = jnp.float32
NL = 16
NY = 4
W = 512
NJ = 32
HALF = NJ // 2
PART = 4
EXTRA = 16
BLOCK = W + EXTRA
TAIL = 128
VMEM = pl.BlockSpec(memory_space=pltpu.VMEM)
SMEM = pl.BlockSpec(memory_space=pltpu.SMEM)
ANY = pl.BlockSpec(memory_space=pl.ANY)
ALONE = pltpu.CompilerParams(vmem_limit_bytes=57 * 1024 * 1024)
PARAMS = pltpu.CompilerParams(vmem_limit_bytes=24 * 1024 * 1024)


def spot(row, y):
    rank = row + (y % 2) * (NL - 1 - 2 * row)
    x, z = rank // 4, rank % 4
    return 4 * x + z + (x % 2) * (3 - 2 * z)


def device_of(row, comp):
    y = row // NL
    return spot(row % NL, y) * 2 * NY + 2 * y + comp


ROWS = NL * NY
CORE = [(device_of(r, c), device_of(r, 1 - c)) for r in range(ROWS) for c in range(2)]
RAISE = [(device_of(r, c), device_of((r + 1) % ROWS, c)) for r in range(ROWS) for c in range(2)]
LOWER = [(device_of(r, c), device_of((r - 1) % ROWS, c)) for r in range(ROWS) for c in range(2)]


def swap(value, pairs):
    return lax.ppermute(value, AXES, pairs)


def exchanges():
    devices = range(NL * 2 * NY)
    even = [(d, d ^ 2) for d in devices]
    odd = [(d, d - d % 8 + (d + (2 if d & 2 else 6)) % 8) for d in devices]
    return [[(d, d ^ 1) for d in devices], even, odd]


def start_all(copies):
    for copy in copies:
        copy.start()
    return copies


def wait_all(copies):
    for copy in copies:
        copy.wait()


def pack_send(place, blocks, send, held, sems):
    entering = start_all([
        pltpu.make_async_copy(blocks.at[0, 1 - place[0], i], held.at[i], sems.at[i]) for i in range(8)
    ])
    leaving = []
    for i in range(8):
        entering[i].wait()
        leaving += start_all([pltpu.make_async_copy(held.at[i], send.at[i], sems.at[8 + i])])
    wait_all(leaving)


def pack_all(place, blocks, extras, received, more, phases, taper, out, phases_out, taper_out, sems):
    core, y = place[0], place[1]
    copies = []
    for i in range(8):
        own, other = spot(8 * core + i, y), spot(8 * (1 - core) + i, y)
        copies += start_all([
            pltpu.make_async_copy(blocks.at[0, core, i], out.at[own, pl.ds(0, W)], sems.at[i]),
            pltpu.make_async_copy(received.at[i], out.at[other, pl.ds(0, W)], sems.at[8 + i]),
        ])
    for i in range(8):
        own, other = spot(8 * core + i, y), spot(8 * (1 - core) + i, y)
        out[own, W:BLOCK, :] = extras[core, i]
        out[other, W:BLOCK, :] = more[i]
    phases_out[...] = phases[...]
    taper_out[...] = taper[...]
    wait_all(copies)


def split_kernel(arrived, *refs):
    parts, sems = refs[:-1], refs[-1]
    wait_all(start_all([
        pltpu.make_async_copy(arrived.at[pl.ds(PART * q, PART)], part, sems.at[q])
        for q, part in enumerate(parts)
    ]))


STEPS = [(layer, False) for layer in range(NL)] + [(layer, True) for layer in range(NL - 2, -1, -1)]


def sweep_kernel(x_steps, y_steps, chunks, place, phases, taper, *refs):
    first = x_steps[0] == 0
    near = () if first else refs[0:2]
    refs = refs[len(near):]
    own_parts, other_parts = refs[:len(chunks)], refs[len(chunks):2 * len(chunks)]
    refs = refs[2 * len(chunks):]
    down, up, send = refs if first else refs[2:]
    columns = lax.broadcasted_iota(jnp.int32, (HALF, W), 1)

    def sweep(core):
        def advance(comp, step, diff):
            layer, is_up = STEPS[step]
            part = (own_parts if comp == core else other_parts)[chunks.index(layer // PART)]
            rows = part[layer % PART, W:BLOCK, :].astype(F32)
            self_coef = rows[8:9] + rows[9:10] + rows[10:11]
            curl_coef = rows[11:12] + rows[12:13] + rows[13:14]

            def solve(vectors):
                return lax.dot_general(
                    vectors.astype(BF16), part[layer % PART, 0:W, :],
                    (((1,), (1,)), ((), ())), preferred_element_type=F32,
                )

            if is_up:
                own = down[comp, layer + 1].astype(F32) if layer == NL - 2 else up[comp, layer + 1]
                current = down[comp, layer].astype(F32) - solve(self_coef * own + curl_coef * diff)
                up[comp, layer] = current
                return current
            shaped = rows[0:8] * taper[...]
            forcing = jnp.concatenate([shaped * phases[layer, 2 * core + m] for m in range(2)], axis=0)
            if layer == 0:
                residue = forcing
            else:
                own = down[comp, layer - 1].astype(F32)
                residue = forcing - (self_coef * own + curl_coef * diff)
            current = solve(residue).astype(BF16)
            down[comp, layer] = current
            current = current.astype(F32)
            if layer == NL - 1:
                up[comp, layer] = current
            return current

        x_new = {}
        for slot, step in enumerate(x_steps):
            diff = None
            if step > 0:
                below = jnp.where(place[2] == 0, 0.0, near[0][slot].astype(F32))
                above = jnp.where(place[2] == ROWS - 1, 0.0, near[1][slot].astype(F32))
                diff = above - below
            x_new[step] = advance(0, step, diff)
        for slot, step in enumerate(y_steps):
            diff = None
            if step > 0:
                field = x_new[step - 1]
                after = jnp.where(columns == W - 1, 0.0, pltpu.roll(field, W - 1, 1))
                before = jnp.where(columns == 0, 0.0, pltpu.roll(field, 1, 1))
                diff = after - before
            send[slot] = advance(1, step, diff).astype(BF16)

    for core in range(2):
        pl.when(place[0] == core)(functools.partial(sweep, core))


def sweep(x_steps, y_steps, place, phases, taper, near, own_parts, other_parts, state):
    x_steps, y_steps = list(x_steps), list(y_steps)
    chunks = sorted({STEPS[step][0] // PART for step in x_steps + y_steps})
    inputs = [taper, *near] + [own_parts[q] for q in chunks] + [other_parts[q] for q in chunks] + list(state)
    aliases = {2 + len(inputs) - len(state) + i: i for i in range(len(state))}
    return pl.pallas_call(
        functools.partial(sweep_kernel, x_steps, y_steps, chunks),
        out_shape=(
            jax.ShapeDtypeStruct((2, NL, HALF, W), BF16),
            jax.ShapeDtypeStruct((2, NL, HALF, W), F32),
            jax.ShapeDtypeStruct((len(y_steps), HALF, W), BF16),
        ),
        in_specs=[SMEM, SMEM] + [VMEM] * len(inputs),
        out_specs=(VMEM, VMEM, VMEM),
        input_output_aliases=aliases,
        compiler_params=PARAMS,
    )(place, phases, *inputs)


def pieces(values):
    out = []
    for _ in range(3):
        part = values.astype(BF16)
        out.append(part)
        values = values - part.astype(F32)
    return out


def share_kernel(place, up, send):
    for layer in range(NL):
        send[layer] = up[1 - place[0], layer].astype(BF16)


def gram_kernel(place, up, received, send):
    core = place[0]
    total = jnp.zeros((NJ, NJ), F32)
    for layer in range(NL):
        own, other = up[core, layer], received[layer].astype(F32)
        low, high = jnp.where(core == 0, own, other), jnp.where(core == 0, other, own)
        rows = jnp.concatenate([low, high], axis=0).astype(BF16)
        total += lax.dot_general(
            rows, rows, (((1,), (1,)), ((), ())), preferred_element_type=F32
        )
        send[layer, :, 0:W] = rows
    tail = jnp.concatenate(pieces(total) + [jnp.zeros((NJ, NJ), BF16)], axis=1)
    for layer in range(NL):
        send[layer, :, W:W + TAIL] = tail


def collect_kernel(place, rows, gram, send):
    total = jnp.zeros((NJ, TAIL), F32)
    for at in range(NL):
        total += rows[at, :, W:W + TAIL].astype(F32)
    gram[...] = total[:, 0:NJ] + total[:, NJ:2 * NJ] + total[:, 2 * NJ:3 * NJ]
    for i in range(8):
        send[i] = rows[spot(8 * (1 - place[0]) + i, place[1]), :, 0:W]


def final_kernel(place, gram, rows, received, out, triangle):
    lane = lax.broadcasted_iota(jnp.int32, (NJ, NJ), 1)
    row = lax.broadcasted_iota(jnp.int32, (NJ, NJ), 0)
    order = jnp.where(lane == (row % 4) * 8 + row // 4, 1.0, 0.0)
    back = jnp.where(row == (lane % 4) * 8 + lane // 4, 1.0, 0.0)
    exact = functools.partial(jnp.dot, precision=lax.Precision.HIGHEST, preferred_element_type=F32)
    left = exact(exact(order, gram[...] * (1.0 / (NL * 2 * ROWS * W))), back)
    right = order
    for k in range(NJ):
        scale = lax.rsqrt(left[k:k + 1, k:k + 1])
        row_left = left[k:k + 1, :] * scale
        row_right = right[k:k + 1, :] * scale
        factor = jnp.where(row > k, left[:, k:k + 1] * scale, 0.0)
        left = jnp.where(row == k, row_left, left - factor * row_left)
        right = jnp.where(row == k, row_right, right - factor * row_right)
    triangle[...] = jnp.where(lane >= row, left, 0.0)
    core, y = place[0], place[1]
    for i in range(8):
        own = exact(right, rows[spot(8 * core + i, y), :, 0:W].astype(F32))
        other = exact(right, received[i].astype(F32))
        out[0, :, 0, i, :] = jnp.where(core == 0, own, other)
        out[0, :, 1, i, :] = jnp.where(core == 0, other, own)


def per_device(source_modes, port_cells, frequencies, layer_inverse, coupling_self, coupling_curl):
    layer_pos = lax.axis_index("layer")
    tile = lax.axis_index("tile")
    core, y = tile % 2, tile // 2
    x, z = layer_pos // 4, layer_pos % 4
    rank = 4 * x + jnp.where(x % 2 == 0, z, 3 - z)
    row = NL * y + jnp.where(y % 2 == 0, rank, NL - 1 - rank)
    place = jnp.stack([core, y, row, jnp.zeros_like(row)]).astype(jnp.int32)

    def split(values):
        out = []
        for _ in range(3):
            part = lax.reduce_precision(values, 8, 7)
            out.append(part.astype(BF16))
            values = values - part
        return out

    extras = jnp.concatenate(
        [jnp.moveaxis(source_modes[0], 0, 2)]
        + [p[:, :, None] for p in split(coupling_self[0]) + split(coupling_curl[0])]
        + [jnp.zeros((2, 8, EXTRA - 14, W), BF16)],
        axis=2,
    )
    columns = jnp.arange(W, dtype=F32)
    offsets = (columns[None, :] - port_cells.astype(F32)[:, None]) / (W // 8)
    port_taper = 1.0 / (1.0 + offsets * offsets)
    angle = frequencies[None, :] * (jnp.arange(NL, dtype=F32)[:, None] + 1.0)
    phases = jnp.stack([jnp.cos(angle), jnp.sin(angle)], axis=2).reshape(NL, 4)
    to_send = pl.pallas_call(
        pack_send,
        out_shape=jax.ShapeDtypeStruct((8, W, W), BF16),
        in_specs=[SMEM, ANY],
        out_specs=ANY,
        scratch_shapes=[pltpu.VMEM((8, W, W), BF16), pltpu.SemaphoreType.DMA((16,))],
        compiler_params=ALONE,
    )(place, layer_inverse)
    received = swap(to_send, CORE)
    more = swap(lax.dynamic_index_in_dim(extras, 1 - core, 0, keepdims=False), CORE)
    packed, phases, port_taper = pl.pallas_call(
        pack_all,
        out_shape=(
            jax.ShapeDtypeStruct((NL, BLOCK, W), BF16),
            jax.ShapeDtypeStruct(phases.shape, F32),
            jax.ShapeDtypeStruct(port_taper.shape, F32),
        ),
        in_specs=[SMEM, ANY, VMEM, ANY, VMEM, VMEM, VMEM],
        out_specs=(VMEM, VMEM, VMEM),
        scratch_shapes=[pltpu.SemaphoreType.DMA((16,))],
        compiler_params=PARAMS,
    )(place, layer_inverse, extras, received, more, phases, port_taper)
    arrived = lax.all_to_all(packed, "layer", 0, 0, tiled=True)

    parts = pl.pallas_call(
        split_kernel,
        out_shape=(jax.ShapeDtypeStruct((PART, BLOCK, W), BF16),) * (NL // PART),
        in_specs=[ANY],
        out_specs=(VMEM,) * (NL // PART),
        scratch_shapes=[pltpu.SemaphoreType.DMA((NL // PART,))],
        compiler_params=PARAMS,
    )(arrived)
    others = [swap(part, CORE) for part in parts]

    run = lambda x_steps, y_steps, near, state: sweep(
        x_steps, y_steps, place, phases, port_taper, near, parts, others, state
    )
    down, up, pair = run(range(1), range(2), (), ())
    last = len(STEPS)
    for at in range(1, last, 2):
        near = (swap(pair, RAISE), swap(pair, LOWER))
        down, up, pair = run(
            range(at, min(at + 2, last)), range(at + 1, min(at + 3, last)), near, (down, up)
        )

    shared = pl.pallas_call(
        share_kernel,
        out_shape=jax.ShapeDtypeStruct((NL, HALF, W), BF16),
        in_specs=[SMEM, VMEM],
        out_specs=VMEM,
        compiler_params=PARAMS,
    )(place, up)
    basis = pl.pallas_call(
        gram_kernel,
        out_shape=jax.ShapeDtypeStruct((NL, NJ, W + TAIL), BF16),
        in_specs=[SMEM, VMEM, VMEM],
        out_specs=VMEM,
        compiler_params=PARAMS,
    )(place, up, swap(shared, CORE))
    rows = lax.all_to_all(basis, "layer", 0, 0, tiled=True)
    gram, back = pl.pallas_call(
        collect_kernel,
        out_shape=(jax.ShapeDtypeStruct((NJ, NJ), F32), jax.ShapeDtypeStruct((8, NJ, W), BF16)),
        in_specs=[SMEM, VMEM],
        out_specs=(VMEM, VMEM),
        compiler_params=PARAMS,
    )(place, rows)
    received = swap(back, CORE)
    for pairs in exchanges():
        gram = gram + swap(gram, pairs)
    out, triangle = pl.pallas_call(
        final_kernel,
        out_shape=(
            jax.ShapeDtypeStruct((1, NJ, 2, 8, W), F32),
            jax.ShapeDtypeStruct((NJ, NJ), F32),
        ),
        in_specs=[SMEM, VMEM, VMEM, VMEM],
        out_specs=(VMEM, VMEM),
        compiler_params=PARAMS,
    )(place, gram, rows, received)
    return (out, triangle)


def solution(mesh):
    in_specs = (
        P("layer", None, None, "tile", None),
        P(),
        P(),
        P("layer", None, "tile", None, None),
        P("layer", None, "tile", None),
        P("layer", None, "tile", None),
    )
    out_specs = (P("layer", None, None, "tile", None), P())
    return jax.shard_map(
        per_device, mesh=mesh, in_specs=in_specs, out_specs=out_specs, check_vma=False
    )
```

```python
import functools

import jax
import jax.numpy as jnp
from jax import lax
from jax.experimental import pallas as pl
from jax.experimental.pallas import tpu as pltpu
from jax.sharding import PartitionSpec as P

AXES = ("layer", "tile")
BF16 = jnp.bfloat16
F32 = jnp.float32
NL = 16
NY = 4
W = 512
NJ = 32
HALF = NJ // 2
BOUNDS = (0, 2, 4, 8, 16)
EXTRA = 16
BLOCK = W + EXTRA
TAIL = 128
VMEM = pl.BlockSpec(memory_space=pltpu.VMEM)
SMEM = pl.BlockSpec(memory_space=pltpu.SMEM)
ANY = pl.BlockSpec(memory_space=pl.ANY)
ALONE = pltpu.CompilerParams(vmem_limit_bytes=57 * 1024 * 1024)
PARAMS = pltpu.CompilerParams(vmem_limit_bytes=24 * 1024 * 1024)


def spot(row, y):
    rank = row + (y % 2) * (NL - 1 - 2 * row)
    x, z = rank // 4, rank % 4
    return 4 * x + z + (x % 2) * (3 - 2 * z)


def device_of(row, comp):
    y = row // NL
    return spot(row % NL, y) * 2 * NY + 2 * y + comp


ROWS = NL * NY
CORE = [(device_of(r, c), device_of(r, 1 - c)) for r in range(ROWS) for c in range(2)]
RAISE = [(device_of(r, c), device_of((r + 1) % ROWS, c)) for r in range(ROWS) for c in range(2)]
LOWER = [(device_of(r, c), device_of((r - 1) % ROWS, c)) for r in range(ROWS) for c in range(2)]


def swap(value, pairs):
    return lax.ppermute(value, AXES, pairs)


def beside_y(by):
    tiles = 2 * NY
    return [(d, d - d % tiles + (d + 2 * by) % tiles) for d in range(NL * tiles)]


def start_all(copies):
    for copy in copies:
        copy.start()
    return copies


def wait_all(copies):
    for copy in copies:
        copy.wait()


def pack_send(blocks, send, held, sems):
    other = 1 - lax.axis_index("tile") % 2
    entering = start_all([
        pltpu.make_async_copy(blocks.at[0, other, i], held.at[i], sems.at[i]) for i in range(8)
    ])
    leaving = []
    for i in range(8):
        entering[i].wait()
        leaving += start_all([pltpu.make_async_copy(held.at[i], send.at[i], sems.at[8 + i])])
    wait_all(leaving)


def pack_own(place, blocks, extras, out, sems):
    core, y = place[0], place[1]
    to = [spot(8 * core + i, y) for i in range(8)]
    copies = start_all([
        pltpu.make_async_copy(blocks.at[0, core, i], out.at[to[i], pl.ds(0, W)], sems.at[i]) for i in range(8)
    ])
    for i in range(8):
        out[to[i], W:BLOCK, :] = extras[core, i]
    wait_all(copies)


def pack_other(place, received, more, phases, taper, part, out, phases_out, taper_out, sems):
    core, y = place[0], place[1]
    to = [spot(8 * (1 - core) + i, y) for i in range(8)]
    copies = start_all([
        pltpu.make_async_copy(received.at[i], out.at[to[i], pl.ds(0, W)], sems.at[i]) for i in range(8)
    ] + [
        pltpu.make_async_copy(more.at[i], out.at[to[i], pl.ds(W, EXTRA)], sems.at[8 + i]) for i in range(8)
    ])
    phases_out[...] = phases[...]
    taper_out[...] = taper[...]
    wait_all(copies)


def part_of(layer):
    return sum(layer >= bound for bound in BOUNDS[1:])


def split_kernel(start, after, arrived, part, sem):
    copy = pltpu.make_async_copy(arrived.at[pl.ds(start, part.shape[0])], part, sem)
    copy.start()
    copy.wait()


STEPS = [(layer, False) for layer in range(NL)] + [(layer, True) for layer in range(NL - 2, -1, -1)]


def sweep_kernel(x_steps, y_steps, chunks, place, phases, taper, *refs):
    first = x_steps[0] == 0
    near = () if first else refs[0:2]
    refs = refs[len(near):]
    own_parts, other_parts = refs[:len(chunks)], refs[len(chunks):2 * len(chunks)]
    refs = refs[2 * len(chunks):]
    down, up, send = refs if first else refs[2:]
    columns = lax.broadcasted_iota(jnp.int32, (HALF, W), 1)

    def sweep(core):
        def advance(comp, step, diff):
            layer, is_up = STEPS[step]
            chunk = part_of(layer)
            part = (own_parts if comp == core else other_parts)[chunks.index(chunk)]
            at = layer - BOUNDS[chunk]
            rows = part[at, W:BLOCK, :].astype(F32)
            self_coef = rows[8:9] + rows[9:10] + rows[10:11]
            curl_coef = rows[11:12] + rows[12:13] + rows[13:14]

            def solve(vectors):
                return lax.dot_general(
                    vectors.astype(BF16), part[at, 0:W, :],
                    (((1,), (1,)), ((), ())), preferred_element_type=F32,
                )

            if is_up:
                own = down[comp, layer + 1].astype(F32) if layer == NL - 2 else up[comp, layer + 1]
                current = down[comp, layer].astype(F32) - solve(self_coef * own + curl_coef * diff)
                up[comp, layer] = current
                return current
            shaped = rows[0:8] * taper[...]
            forcing = jnp.concatenate([shaped * phases[layer, 2 * core + m] for m in range(2)], axis=0)
            if layer == 0:
                residue = forcing
            else:
                own = down[comp, layer - 1].astype(F32)
                residue = forcing - (self_coef * own + curl_coef * diff)
            current = solve(residue).astype(BF16)
            down[comp, layer] = current
            current = current.astype(F32)
            if layer == NL - 1:
                up[comp, layer] = current
            return current

        x_new = {}
        for slot, step in enumerate(x_steps):
            diff = None
            if step > 0:
                below = jnp.where(place[2] == 0, 0.0, near[0][slot].astype(F32))
                above = jnp.where(place[2] == ROWS - 1, 0.0, near[1][slot].astype(F32))
                diff = above - below
            x_new[step] = advance(0, step, diff)
        for slot, step in enumerate(y_steps):
            diff = None
            if step > 0:
                field = x_new[step - 1]
                after = jnp.where(columns == W - 1, 0.0, pltpu.roll(field, W - 1, 1))
                before = jnp.where(columns == 0, 0.0, pltpu.roll(field, 1, 1))
                diff = after - before
            send[slot] = advance(1, step, diff).astype(BF16)

    for core in range(2):
        pl.when(place[0] == core)(functools.partial(sweep, core))


def sweep(x_steps, y_steps, place, phases, taper, near, own_parts, other_parts, state):
    x_steps, y_steps = list(x_steps), list(y_steps)
    chunks = sorted({part_of(STEPS[step][0]) for step in x_steps + y_steps})
    inputs = [taper, *near] + [own_parts[q] for q in chunks] + [other_parts[q] for q in chunks] + list(state)
    aliases = {2 + len(inputs) - len(state) + i: i for i in range(len(state))}
    return pl.pallas_call(
        functools.partial(sweep_kernel, x_steps, y_steps, chunks),
        out_shape=(
            jax.ShapeDtypeStruct((2, NL, HALF, W), BF16),
            jax.ShapeDtypeStruct((2, NL, HALF, W), F32),
            jax.ShapeDtypeStruct((len(y_steps), HALF, W), BF16),
        ),
        in_specs=[SMEM, SMEM] + [VMEM] * len(inputs),
        out_specs=(VMEM, VMEM, VMEM),
        input_output_aliases=aliases,
        compiler_params=PARAMS,
    )(place, phases, *inputs)


def pieces(values):
    out = []
    for _ in range(3):
        part = values.astype(BF16)
        out.append(part)
        values = values - part.astype(F32)
    return out


def share_kernel(place, up, send):
    for layer in range(NL):
        send[layer] = up[1 - place[0], layer].astype(BF16)


def gram_kernel(place, up, received, send):
    core = place[0]
    total = jnp.zeros((NJ, NJ), F32)
    for layer in range(NL):
        own, other = up[core, layer], received[layer].astype(F32)
        low, high = jnp.where(core == 0, own, other), jnp.where(core == 0, other, own)
        rows = jnp.concatenate([low, high], axis=0).astype(BF16)
        total += lax.dot_general(
            rows, rows, (((1,), (1,)), ((), ())), preferred_element_type=F32
        )
        send[layer, :, 0:W] = rows
    tail = jnp.concatenate(pieces(total) + [jnp.zeros((NJ, NJ), BF16)], axis=1)
    for layer in range(NL):
        send[layer, :, W:W + TAIL] = tail


def collect_kernel(place, rows, gram, send):
    total = jnp.zeros((NJ, TAIL), F32)
    for at in range(NL):
        total += rows[at, :, W:W + TAIL].astype(F32)
    gram[...] = total[:, 0:NJ] + total[:, NJ:2 * NJ] + total[:, 2 * NJ:3 * NJ]
    for i in range(8):
        send[i] = rows[spot(8 * (1 - place[0]) + i, place[1]), :, 0:W]


def final_kernel(place, gram_0, gram_2, gram_1, gram_3, rows, received, out, triangle):
    lane = lax.broadcasted_iota(jnp.int32, (NJ, NJ), 1)
    row = lax.broadcasted_iota(jnp.int32, (NJ, NJ), 0)
    order = jnp.where(lane == (row % 4) * 8 + row // 4, 1.0, 0.0)
    back = jnp.where(row == (lane % 4) * 8 + lane // 4, 1.0, 0.0)
    exact = functools.partial(jnp.dot, precision=lax.Precision.HIGHEST, preferred_element_type=F32)
    gram = (gram_0[...] + gram_2[...]) + (gram_1[...] + gram_3[...])
    left = exact(exact(order, gram * (1.0 / (NL * 2 * ROWS * W))), back)
    both = jnp.concatenate([left, order], axis=1)
    wide_row = lax.broadcasted_iota(jnp.int32, both.shape, 0)
    wide_lane = lax.broadcasted_iota(jnp.int32, both.shape, 1)
    for k in range(NJ):
        factor = both[:, k:k + 1] * (1.0 / both[k:k + 1, k:k + 1])
        both = both - jnp.where(wide_row > k, factor, 0.0) * both[k:k + 1, :]
    pivots = jnp.sum(jnp.where(wide_lane == wide_row, both, 0.0), axis=1, keepdims=True)
    both = both * lax.rsqrt(pivots)
    triangle[...] = jnp.where(lane >= row, both[:, 0:NJ], 0.0)
    inverse = jnp.concatenate(pieces(both[:, NJ:2 * NJ]), axis=0)

    def product(values):
        thirds = jnp.dot(inverse, values, preferred_element_type=F32)
        return thirds[0:NJ] + thirds[NJ:2 * NJ] + thirds[2 * NJ:3 * NJ]

    core, y = place[0], place[1]
    for i in range(8):
        own = product(rows[spot(8 * core + i, y), :, 0:W])
        other = product(received[i])
        out[0, :, 0, i, :] = jnp.where(core == 0, own, other)
        out[0, :, 1, i, :] = jnp.where(core == 0, other, own)


def per_device(source_modes, port_cells, frequencies, layer_inverse, coupling_self, coupling_curl):
    layer_pos = lax.axis_index("layer")
    tile = lax.axis_index("tile")
    core, y = tile % 2, tile // 2
    x, z = layer_pos // 4, layer_pos % 4
    rank = 4 * x + jnp.where(x % 2 == 0, z, 3 - z)
    row = NL * y + jnp.where(y % 2 == 0, rank, NL - 1 - rank)
    place = jnp.stack([core, y, row, jnp.zeros_like(row)]).astype(jnp.int32)

    def split(values):
        out = []
        for _ in range(3):
            part = lax.reduce_precision(values, 8, 7)
            out.append(part.astype(BF16))
            values = values - part
        return out

    extras = jnp.concatenate(
        [jnp.moveaxis(source_modes[0], 0, 2)]
        + [p[:, :, None] for p in split(coupling_self[0]) + split(coupling_curl[0])]
        + [jnp.zeros((2, 8, EXTRA - 14, W), BF16)],
        axis=2,
    )
    columns = jnp.arange(W, dtype=F32)
    offsets = (columns[None, :] - port_cells.astype(F32)[:, None]) / (W // 8)
    port_taper = 1.0 / (1.0 + offsets * offsets)
    angle = frequencies[None, :] * (jnp.arange(NL, dtype=F32)[:, None] + 1.0)
    phases = jnp.stack([jnp.cos(angle), jnp.sin(angle)], axis=2).reshape(NL, 4)
    to_send = pl.pallas_call(
        pack_send,
        out_shape=jax.ShapeDtypeStruct((8, W, W), BF16),
        in_specs=[ANY],
        out_specs=ANY,
        scratch_shapes=[pltpu.VMEM((8, W, W), BF16), pltpu.SemaphoreType.DMA((16,))],
        compiler_params=ALONE,
    )(layer_inverse)
    received = swap(to_send, CORE)
    more = swap(lax.dynamic_index_in_dim(extras, 1 - core, 0, keepdims=False), CORE)
    part = pl.pallas_call(
        pack_own,
        out_shape=jax.ShapeDtypeStruct((NL, BLOCK, W), BF16),
        in_specs=[SMEM, ANY, VMEM],
        out_specs=VMEM,
        scratch_shapes=[pltpu.SemaphoreType.DMA((8,))],
        compiler_params=PARAMS,
    )(place, layer_inverse, extras)
    packed, phases, port_taper = pl.pallas_call(
        pack_other,
        out_shape=(
            jax.ShapeDtypeStruct((NL, BLOCK, W), BF16),
            jax.ShapeDtypeStruct(phases.shape, F32),
            jax.ShapeDtypeStruct(port_taper.shape, F32),
        ),
        in_specs=[SMEM, VMEM, VMEM, VMEM, VMEM, ANY],
        out_specs=(ANY, VMEM, VMEM),
        input_output_aliases={5: 0},
        scratch_shapes=[pltpu.SemaphoreType.DMA((16,))],
        compiler_params=PARAMS,
    )(place, received, more, phases, port_taper, part)
    arrived = lax.all_to_all(packed, "layer", 0, 0, tiled=True)

    parts, others = [], []

    def trade(after):
        start, end = BOUNDS[len(parts):len(parts) + 2]
        part = pl.pallas_call(
            functools.partial(split_kernel, start),
            out_shape=jax.ShapeDtypeStruct((end - start, BLOCK, W), BF16),
            in_specs=[ANY, ANY],
            out_specs=VMEM,
            scratch_shapes=[pltpu.SemaphoreType.DMA],
            compiler_params=PARAMS,
        )(after, arrived)
        parts.append(part)
        others.append(swap(part, CORE))

    run = lambda x_steps, y_steps, near, state: sweep(
        x_steps, y_steps, place, phases, port_taper, near, parts, others, state
    )
    trade(port_taper)
    down, up, pair = run(range(1), range(2), (), ())
    last = len(STEPS)
    for at in range(1, last, 2):
        near = (swap(pair, RAISE), swap(pair, LOWER))
        if len(parts) < len(BOUNDS) - 1:
            trade(pair)
        down, up, pair = run(
            range(at, min(at + 2, last)), range(at + 1, min(at + 3, last)), near, (down, up)
        )

    shared = pl.pallas_call(
        share_kernel,
        out_shape=jax.ShapeDtypeStruct((NL, HALF, W), BF16),
        in_specs=[SMEM, VMEM],
        out_specs=VMEM,
        compiler_params=PARAMS,
    )(place, up)
    basis = pl.pallas_call(
        gram_kernel,
        out_shape=jax.ShapeDtypeStruct((NL, NJ, W + TAIL), BF16),
        in_specs=[SMEM, VMEM, VMEM],
        out_specs=VMEM,
        compiler_params=PARAMS,
    )(place, up, swap(shared, CORE))
    rows = lax.all_to_all(basis, "layer", 0, 0, tiled=True)
    gram, back = pl.pallas_call(
        collect_kernel,
        out_shape=(jax.ShapeDtypeStruct((NJ, NJ), F32), jax.ShapeDtypeStruct((8, NJ, W), BF16)),
        in_specs=[SMEM, VMEM],
        out_specs=(VMEM, VMEM),
        compiler_params=PARAMS,
    )(place, rows)
    received = swap(back, CORE)
    gram = gram + swap(gram, CORE)
    grams = [gram] + [swap(gram, beside_y(by)) for by in (2, 1, 3)]
    out, triangle = pl.pallas_call(
        final_kernel,
        out_shape=(
            jax.ShapeDtypeStruct((1, NJ, 2, 8, W), F32),
            jax.ShapeDtypeStruct((NJ, NJ), F32),
        ),
        in_specs=[SMEM] + [VMEM] * 6,
        out_specs=(VMEM, VMEM),
        compiler_params=PARAMS,
    )(place, *grams, rows, received)
    return (out, triangle)


def solution(mesh):
    in_specs = (
        P("layer", None, None, "tile", None),
        P(),
        P(),
        P("layer", None, "tile", None, None),
        P("layer", None, "tile", None),
        P("layer", None, "tile", None),
    )
    out_specs = (P("layer", None, None, "tile", None), P())
    return jax.shard_map(
        per_device, mesh=mesh, in_specs=in_specs, out_specs=out_specs, check_vma=False
    )
```

```python
import functools

import jax
import jax.numpy as jnp
from jax import lax
from jax.experimental import pallas as pl
from jax.experimental.pallas import tpu as pltpu
from jax.sharding import PartitionSpec as P

AXES = ("layer", "tile")
BF16 = jnp.bfloat16
F32 = jnp.float32
NL = 16
NY = 4
W = 512
NJ = 32
HALF = NJ // 2
LATE = 2
SENT = 4
BOUNDS = (0, 2, 4, 8, 16)
EXTRA = 16
BLOCK = W + EXTRA
TAIL = 128
VMEM = pl.BlockSpec(memory_space=pltpu.VMEM)
SMEM = pl.BlockSpec(memory_space=pltpu.SMEM)
ANY = pl.BlockSpec(memory_space=pl.ANY)
ALONE = pltpu.CompilerParams(vmem_limit_bytes=57 * 1024 * 1024)
PARAMS = pltpu.CompilerParams(vmem_limit_bytes=24 * 1024 * 1024)


def spot(row, y):
    rank = row + (y % 2) * (NL - 1 - 2 * row)
    x, z = rank // 4, rank % 4
    return 4 * x + z + (x % 2) * (3 - 2 * z)


def device_of(row, comp):
    y = row // NL
    return spot(row % NL, y) * 2 * NY + 2 * y + comp


ROWS = NL * NY
CORE = [(device_of(r, c), device_of(r, 1 - c)) for r in range(ROWS) for c in range(2)]
RAISE = [(device_of(r, c), device_of((r + 1) % ROWS, c)) for r in range(ROWS) for c in range(2)]
LOWER = [(device_of(r, c), device_of((r - 1) % ROWS, c)) for r in range(ROWS) for c in range(2)]


def swap(value, pairs):
    return lax.ppermute(value, AXES, pairs)


def beside_y(by):
    tiles = 2 * NY
    return [(d, d - d % tiles + (d + 2 * by) % tiles) for d in range(NL * tiles)]


def start_all(copies):
    for copy in copies:
        copy.start()
    return copies


def wait_all(copies):
    for copy in copies:
        copy.wait()


def pack_send(first, blocks, send, held, sems):
    other = 1 - lax.axis_index("tile") % 2
    entering = start_all([
        pltpu.make_async_copy(blocks.at[0, other, first + i], held.at[i], sems.at[i]) for i in range(SENT)
    ])
    leaving = []
    for i in range(SENT):
        entering[i].wait()
        leaving += start_all([pltpu.make_async_copy(held.at[i], send.at[i], sems.at[SENT + i])])
    wait_all(leaving)


def pack_own(place, blocks, extras, out, sems):
    core, y = place[0], place[1]
    to = [spot(8 * core + i, y) for i in range(8)]
    copies = start_all([
        pltpu.make_async_copy(blocks.at[0, core, i], out.at[to[i], pl.ds(0, W)], sems.at[i]) for i in range(8)
    ])
    for i in range(8):
        out[to[i], W:BLOCK, :] = extras[core, i]
    wait_all(copies)


def pack_other(place, received_0, received_1, more, phases, taper, part, out, phases_out, taper_out, sems):
    core, y = place[0], place[1]
    to = [spot(8 * (1 - core) + i, y) for i in range(8)]
    copies = start_all([
        pltpu.make_async_copy(received.at[i], out.at[to[at + i], pl.ds(0, W)], sems.at[at + i])
        for at, received in ((0, received_0), (SENT, received_1)) for i in range(SENT)
    ] + [
        pltpu.make_async_copy(more.at[i], out.at[to[i], pl.ds(W, EXTRA)], sems.at[8 + i]) for i in range(8)
    ])
    phases_out[...] = phases[...]
    taper_out[...] = taper[...]
    wait_all(copies)


def part_of(layer):
    return sum(layer >= bound for bound in BOUNDS[1:])


def split_kernel(start, after, arrived, part, sem):
    copy = pltpu.make_async_copy(arrived.at[pl.ds(start, part.shape[0])], part, sem)
    copy.start()
    copy.wait()


STEPS = [(layer, False) for layer in range(NL)] + [(layer, True) for layer in range(NL - 2, -1, -1)]


def sweep_kernel(x_steps, y_steps, chunks, place, phases, taper, *refs):
    first = x_steps[0] == 0
    near = () if first else refs[0:2]
    refs = refs[len(near):]
    own_parts, other_parts = refs[:len(chunks)], refs[len(chunks):2 * len(chunks)]
    refs = refs[2 * len(chunks):]
    down, up, send = refs if first else refs[2:]
    columns = lax.broadcasted_iota(jnp.int32, (HALF, W), 1)

    def sweep(core):
        def advance(comp, step, diff):
            layer, is_up = STEPS[step]
            chunk = part_of(layer)
            part = (own_parts if comp == core else other_parts)[chunks.index(chunk)]
            at = layer - BOUNDS[chunk]
            rows = part[at, W:BLOCK, :].astype(F32)
            self_coef = rows[8:9] + rows[9:10] + rows[10:11]
            curl_coef = rows[11:12] + rows[12:13] + rows[13:14]

            def solve(vectors):
                return lax.dot_general(
                    vectors.astype(BF16), part[at, 0:W, :],
                    (((1,), (1,)), ((), ())), preferred_element_type=F32,
                )

            if is_up:
                own = down[comp, layer + 1].astype(F32) if layer == NL - 2 else up[comp, layer + 1]
                current = down[comp, layer].astype(F32) - solve(self_coef * own + curl_coef * diff)
                up[comp, layer] = current
                return current
            shaped = rows[0:8] * taper[...]
            forcing = jnp.concatenate([shaped * phases[layer, 2 * core + m] for m in range(2)], axis=0)
            if layer == 0:
                residue = forcing
            else:
                own = down[comp, layer - 1].astype(F32)
                residue = forcing - (self_coef * own + curl_coef * diff)
            current = solve(residue).astype(BF16)
            down[comp, layer] = current
            current = current.astype(F32)
            if layer == NL - 1:
                up[comp, layer] = current
            return current

        x_new = {}
        for slot, step in enumerate(x_steps):
            diff = None
            if step > 0:
                below = jnp.where(place[2] == 0, 0.0, near[0][slot].astype(F32))
                above = jnp.where(place[2] == ROWS - 1, 0.0, near[1][slot].astype(F32))
                diff = above - below
            x_new[step] = advance(0, step, diff)
        for slot, step in enumerate(y_steps):
            diff = None
            if step > 0:
                field = x_new[step - 1]
                after = jnp.where(columns == W - 1, 0.0, pltpu.roll(field, W - 1, 1))
                before = jnp.where(columns == 0, 0.0, pltpu.roll(field, 1, 1))
                diff = after - before
            send[slot] = advance(1, step, diff).astype(BF16)

    for core in range(2):
        pl.when(place[0] == core)(functools.partial(sweep, core))


def sweep(x_steps, y_steps, place, phases, taper, near, own_parts, other_parts, state):
    x_steps, y_steps = list(x_steps), list(y_steps)
    chunks = sorted({part_of(STEPS[step][0]) for step in x_steps + y_steps})
    inputs = [taper, *near] + [own_parts[q] for q in chunks] + [other_parts[q] for q in chunks] + list(state)
    aliases = {2 + len(inputs) - len(state) + i: i for i in range(len(state))}
    return pl.pallas_call(
        functools.partial(sweep_kernel, x_steps, y_steps, chunks),
        out_shape=(
            jax.ShapeDtypeStruct((2, NL, HALF, W), BF16),
            jax.ShapeDtypeStruct((2, NL, HALF, W), F32),
            jax.ShapeDtypeStruct((len(y_steps), HALF, W), BF16),
        ),
        in_specs=[SMEM, SMEM] + [VMEM] * len(inputs),
        out_specs=(VMEM, VMEM, VMEM),
        input_output_aliases=aliases,
        compiler_params=PARAMS,
    )(place, phases, *inputs)


def pieces(values):
    out = []
    for _ in range(3):
        part = values.astype(BF16)
        out.append(part)
        values = values - part.astype(F32)
    return out


def share_kernel(start, place, up, send):
    for at in range(send.shape[0]):
        send[at] = up[1 - place[0], start + at].astype(BF16)


def gram_kernel(place, up, late, early, send):
    core = place[0]
    total = jnp.zeros((NJ, NJ), F32)
    for layer in range(NL):
        own = up[core, layer]
        other = (late[layer] if layer < LATE else early[layer - LATE]).astype(F32)
        low, high = jnp.where(core == 0, own, other), jnp.where(core == 0, other, own)
        rows = jnp.concatenate([low, high], axis=0).astype(BF16)
        total += lax.dot_general(
            rows, rows, (((1,), (1,)), ((), ())), preferred_element_type=F32
        )
        send[layer, :, 0:W] = rows
    tail = jnp.concatenate(pieces(total) + [jnp.zeros((NJ, NJ), BF16)], axis=1)
    for layer in range(NL):
        send[layer, :, W:W + TAIL] = tail


def collect_kernel(place, rows, gram, send):
    total = jnp.zeros((NJ, TAIL), F32)
    for at in range(NL):
        total += rows[at, :, W:W + TAIL].astype(F32)
    gram[...] = total[:, 0:NJ] + total[:, NJ:2 * NJ] + total[:, 2 * NJ:3 * NJ]
    for i in range(8):
        send[i] = rows[spot(8 * (1 - place[0]) + i, place[1]), :, 0:W]


def final_kernel(place, gram_0, gram_2, gram_1, gram_3, rows, received, out, triangle):
    lane = lax.broadcasted_iota(jnp.int32, (NJ, NJ), 1)
    row = lax.broadcasted_iota(jnp.int32, (NJ, NJ), 0)
    order = jnp.where(lane == (row % 4) * 8 + row // 4, 1.0, 0.0)
    back = jnp.where(row == (lane % 4) * 8 + lane // 4, 1.0, 0.0)
    exact = functools.partial(jnp.dot, precision=lax.Precision.HIGHEST, preferred_element_type=F32)
    gram = (gram_0[...] + gram_2[...]) + (gram_1[...] + gram_3[...])
    left = exact(exact(order, gram * (1.0 / (NL * 2 * ROWS * W))), back)
    both = jnp.concatenate([left, order], axis=1)
    wide_row = lax.broadcasted_iota(jnp.int32, both.shape, 0)
    wide_lane = lax.broadcasted_iota(jnp.int32, both.shape, 1)
    for k in range(NJ):
        factor = both[:, k:k + 1] * (1.0 / both[k:k + 1, k:k + 1])
        both = both - jnp.where(wide_row > k, factor, 0.0) * both[k:k + 1, :]
    pivots = jnp.sum(jnp.where(wide_lane == wide_row, both, 0.0), axis=1, keepdims=True)
    both = both * lax.rsqrt(pivots)
    triangle[...] = jnp.where(lane >= row, both[:, 0:NJ], 0.0)
    inverse = jnp.concatenate(pieces(both[:, NJ:2 * NJ]), axis=0)

    def product(values):
        thirds = jnp.dot(inverse, values, preferred_element_type=F32)
        return thirds[0:NJ] + thirds[NJ:2 * NJ] + thirds[2 * NJ:3 * NJ]

    core, y = place[0], place[1]
    for i in range(8):
        own = product(rows[spot(8 * core + i, y), :, 0:W])
        other = product(received[i])
        out[0, :, 0, i, :] = jnp.where(core == 0, own, other)
        out[0, :, 1, i, :] = jnp.where(core == 0, other, own)


def per_device(source_modes, port_cells, frequencies, layer_inverse, coupling_self, coupling_curl):
    layer_pos = lax.axis_index("layer")
    tile = lax.axis_index("tile")
    core, y = tile % 2, tile // 2
    x, z = layer_pos // 4, layer_pos % 4
    rank = 4 * x + jnp.where(x % 2 == 0, z, 3 - z)
    row = NL * y + jnp.where(y % 2 == 0, rank, NL - 1 - rank)
    place = jnp.stack([core, y, row, jnp.zeros_like(row)]).astype(jnp.int32)

    def split(values):
        out = []
        for _ in range(3):
            part = lax.reduce_precision(values, 8, 7)
            out.append(part.astype(BF16))
            values = values - part
        return out

    extras = jnp.concatenate(
        [jnp.moveaxis(source_modes[0], 0, 2)]
        + [p[:, :, None] for p in split(coupling_self[0]) + split(coupling_curl[0])]
        + [jnp.zeros((2, 8, EXTRA - 14, W), BF16)],
        axis=2,
    )
    columns = jnp.arange(W, dtype=F32)
    offsets = (columns[None, :] - port_cells.astype(F32)[:, None]) / (W // 8)
    port_taper = 1.0 / (1.0 + offsets * offsets)
    angle = frequencies[None, :] * (jnp.arange(NL, dtype=F32)[:, None] + 1.0)
    phases = jnp.stack([jnp.cos(angle), jnp.sin(angle)], axis=2).reshape(NL, 4)
    received = [
        swap(
            pl.pallas_call(
                functools.partial(pack_send, first),
                out_shape=jax.ShapeDtypeStruct((SENT, W, W), BF16),
                in_specs=[ANY],
                out_specs=ANY,
                scratch_shapes=[pltpu.VMEM((SENT, W, W), BF16), pltpu.SemaphoreType.DMA((2 * SENT,))],
                compiler_params=ALONE,
            )(layer_inverse),
            CORE,
        )
        for first in (0, SENT)
    ]
    more = swap(lax.dynamic_index_in_dim(extras, 1 - core, 0, keepdims=False), CORE)
    part = pl.pallas_call(
        pack_own,
        out_shape=jax.ShapeDtypeStruct((NL, BLOCK, W), BF16),
        in_specs=[SMEM, ANY, VMEM],
        out_specs=VMEM,
        scratch_shapes=[pltpu.SemaphoreType.DMA((8,))],
        compiler_params=PARAMS,
    )(place, layer_inverse, extras)
    packed, phases, port_taper = pl.pallas_call(
        pack_other,
        out_shape=(
            jax.ShapeDtypeStruct((NL, BLOCK, W), BF16),
            jax.ShapeDtypeStruct(phases.shape, F32),
            jax.ShapeDtypeStruct(port_taper.shape, F32),
        ),
        in_specs=[SMEM] + [VMEM] * 5 + [ANY],
        out_specs=(ANY, VMEM, VMEM),
        input_output_aliases={6: 0},
        scratch_shapes=[pltpu.SemaphoreType.DMA((16,))],
        compiler_params=PARAMS,
    )(place, *received, more, phases, port_taper, part)
    arrived = lax.all_to_all(packed, "layer", 0, 0, tiled=True)

    parts, others = [], []

    def trade(after):
        start, end = BOUNDS[len(parts):len(parts) + 2]
        part = pl.pallas_call(
            functools.partial(split_kernel, start),
            out_shape=jax.ShapeDtypeStruct((end - start, BLOCK, W), BF16),
            in_specs=[ANY, ANY],
            out_specs=VMEM,
            scratch_shapes=[pltpu.SemaphoreType.DMA],
            compiler_params=PARAMS,
        )(after, arrived)
        parts.append(part)
        others.append(swap(part, CORE))

    run = lambda x_steps, y_steps, near, state: sweep(
        x_steps, y_steps, place, phases, port_taper, near, parts, others, state
    )
    def share(up, start, end):
        return pl.pallas_call(
            functools.partial(share_kernel, start),
            out_shape=jax.ShapeDtypeStruct((end - start, HALF, W), BF16),
            in_specs=[SMEM, VMEM],
            out_specs=VMEM,
            compiler_params=PARAMS,
        )(place, up)

    trade(port_taper)
    down, up, pair = run(range(1), range(2), (), ())
    last = len(STEPS)
    for at in range(1, last, 2):
        near = (swap(pair, RAISE), swap(pair, LOWER))
        if len(parts) < len(BOUNDS) - 1:
            trade(pair)
        if at + 2 == last:
            early = swap(share(up, LATE, NL), CORE)
        down, up, pair = run(
            range(at, min(at + 2, last)), range(at + 1, min(at + 3, last)), near, (down, up)
        )

    late = swap(share(up, 0, LATE), CORE)
    basis = pl.pallas_call(
        gram_kernel,
        out_shape=jax.ShapeDtypeStruct((NL, NJ, W + TAIL), BF16),
        in_specs=[SMEM, VMEM, VMEM, VMEM],
        out_specs=VMEM,
        compiler_params=PARAMS,
    )(place, up, late, early)
    rows = lax.all_to_all(basis, "layer", 0, 0, tiled=True)
    gram, back = pl.pallas_call(
        collect_kernel,
        out_shape=(jax.ShapeDtypeStruct((NJ, NJ), F32), jax.ShapeDtypeStruct((8, NJ, W), BF16)),
        in_specs=[SMEM, VMEM],
        out_specs=(VMEM, VMEM),
        compiler_params=PARAMS,
    )(place, rows)
    received = swap(back, CORE)
    gram = gram + swap(gram, CORE)
    grams = [gram] + [swap(gram, beside_y(by)) for by in (2, 1, 3)]
    out, triangle = pl.pallas_call(
        final_kernel,
        out_shape=(
            jax.ShapeDtypeStruct((1, NJ, 2, 8, W), F32),
            jax.ShapeDtypeStruct((NJ, NJ), F32),
        ),
        in_specs=[SMEM] + [VMEM] * 6,
        out_specs=(VMEM, VMEM),
        compiler_params=PARAMS,
    )(place, *grams, rows, received)
    return (out, triangle)


def solution(mesh):
    in_specs = (
        P("layer", None, None, "tile", None),
        P(),
        P(),
        P("layer", None, "tile", None, None),
        P("layer", None, "tile", None),
        P("layer", None, "tile", None),
    )
    out_specs = (P("layer", None, None, "tile", None), P())
    return jax.shard_map(
        per_device, mesh=mesh, in_specs=in_specs, out_specs=out_specs, check_vma=False
    )
```
